256 devices in a mesh: kv: 64 (over y, z, core), tp: 4 (over x).
Axes of the slice: x: 4, y: 4, z: 8, core: 2. Of those that a mesh axis runs over, the one named last changes fastest.
Arguments:
- query: bfloat16 [16, 128, 128], P(None, 'tp'), may hold values from -128 to 128
- key_cache: bfloat16 [16, 32768, 8, 128], P(None, 'kv', 'tp'), may hold values from -4 to 4
- value_cache: bfloat16 [16, 32768, 8, 128], P(None, 'kv', 'tp'), may hold values from -6 to 6
- lengths: int32 [16], replicated, may hold values from 4096 to 32768, as said below
- out_weight: bfloat16 [128, 128, 16384], P('tp', 'kv'), may hold values from -0.046875 to 0.046875
Outputs:
- projected: bfloat16 [16, 16384], P(None, ('kv', 'tp'))
The draws below stay inside these ranges and needn't reach their ends.
Inputs may be any that keep to these rules, and one draw needn't show every extreme that they name: lengths[0] is 32768.
All inputs are finite; a program needn't handle non-finite values.
Results may differ from the reference program's by a relative error of at most 0.007.
Values may be sent and summed in bfloat16 or wider, within the bound.
No kernel may reach another device: no remote copies, remote signals or barrier semaphores. Data moves between devices by JAX's collectives and lax.ppermute only.
A program may use at most 128 MiB of HBM per device.

```python
import jax
import jax.numpy as jnp
from jax import lax

D = 16384
HQ = 128
KVH = 8
HD = 128
SEQS = 16
POS_DEV = 512
CTX = 32768
N_KV = 64


def shared_keys(key):
    return jax.random.truncated_normal(key, -4.0, 4.0, (SEQS, CTX, KVH, HD), jnp.float32)


def draw_key_cache(key, part):
    keys = shared_keys(key)
    return keys.astype(jnp.bfloat16)


def draw_query(key, part):
    key = jax.random.fold_in(key, 7)
    entries = jax.random.truncated_normal(key, -4.0, 4.0, (SEQS, HQ, HD), jnp.float32)
    return entries.astype(jnp.bfloat16)


def draw_lengths(key, part):
    key = jax.random.fold_in(key, 11)
    drawn = jax.random.randint(key, (SEQS,), CTX // 8, CTX + 1, dtype=jnp.int32)
    return drawn.at[0].set(CTX)


def shard_levels(own_key, dims, pieces, least, top_value):
    gain = 1.0
    for dim, blocks in pieces:
        draws = jax.random.uniform(jax.random.fold_in(jax.random.fold_in(own_key, 6), dim), (blocks,), jnp.float32, least / len(pieces), top_value / len(pieces))
        gain = gain * jnp.repeat(jnp.exp(draws), dims[dim] // blocks).reshape((-1,) + (1,) * (len(dims) - 1 - dim))
    return gain


def scatter_about(rng, extent, spread, limit, pieces=(), kind=jnp.bfloat16):
    values = spread * jax.random.normal(rng, extent, jnp.float32)
    if pieces:
        values = values * shard_levels(rng, extent, pieces, -0.22, 0.18)
    return jnp.clip(values, -limit, limit).astype(kind)


def setup_inputs(seed: int = 0) -> dict:
    seeds = jax.random.split(jax.random.key(seed), 6)
    query = draw_query(jax.random.fold_in(seeds[5], 71), 0)
    key_cache = draw_key_cache(jax.random.fold_in(seeds[5], 71), 0)
    value_cache = scatter_about(seeds[2], (SEQS, CTX, KVH, HD), 1.0, 6.0, ((1, 64), (2, 4)))
    lengths = draw_lengths(jax.random.fold_in(seeds[5], 71), 0)
    out_weight = scatter_about(seeds[4], (HQ, HD, D), (HQ * HD) ** -0.5, 0.046875, ((0, 4), (1, 64)))
    return dict(query=query, key_cache=key_cache, value_cache=value_cache, lengths=lengths, out_weight=out_weight)


def block_part(query, keys, values, live):
    group = HQ // KVH
    grouped = query.astype(jnp.float32).reshape(SEQS, KVH, group, HD)
    scores = jnp.einsum('bgqd,bpgd->bgqp', grouped, keys.astype(jnp.float32)) / jnp.sqrt(jnp.float32(HD))
    mask = live[:, None, None, :]
    masked = jnp.where(mask, scores, jnp.float32(-1e+30))
    block_max = lax.optimization_barrier(jnp.max(masked, axis=-1))
    weights = jnp.where(mask, jnp.exp(scores - block_max[..., None]), jnp.float32(0.0))
    block_total = lax.optimization_barrier(jnp.sum(weights, axis=-1))
    weight_bf = weights.astype(jnp.bfloat16)
    summed = jnp.einsum('bgqp,bpgd->bgqd', weight_bf.astype(jnp.float32), values.astype(jnp.float32))
    floored = jnp.maximum(block_total, jnp.float32(1.0))
    block_out = (summed / floored[..., None]).astype(jnp.bfloat16).reshape(SEQS, HQ, HD)
    block_lse = (block_max + jnp.log(floored)).reshape(SEQS, HQ)
    return (block_out, block_lse)

def reference(query, key_cache, value_cache, lengths, out_weight):

    def one_block(index):
        start = (index * POS_DEV).astype(jnp.int32)
        keys = lax.dynamic_slice_in_dim(key_cache, start, POS_DEV, 1)
        values = lax.dynamic_slice_in_dim(value_cache, start, POS_DEV, 1)
        positions = start + jnp.arange(POS_DEV, dtype=jnp.int32)
        live = positions[None, :] < lengths[:, None]
        return block_part(query, keys, values, live)
    outs_all, lse_all = lax.map(one_block, jnp.arange(N_KV, dtype=jnp.int32))
    highest = lax.optimization_barrier(jnp.max(lse_all, axis=0))
    scales = jnp.exp(lse_all - highest[None])
    merged = lax.optimization_barrier(jnp.sum(scales[..., None] * outs_all.astype(jnp.float32), axis=0)) / lax.optimization_barrier(jnp.sum(scales, axis=0))[..., None]
    merged = merged.astype(jnp.bfloat16).reshape(SEQS, HQ * HD)
    projected = jnp.dot(merged, out_weight.reshape(HQ * HD, D), preferred_element_type=jnp.float32)
    return projected.astype(jnp.bfloat16)
```

```python
import functools

import jax
import jax.numpy as jnp
import numpy as np
from jax import lax
from jax.experimental import pallas as pl
from jax.experimental.pallas import tpu as pltpu
from jax.sharding import Mesh
from jax.sharding import PartitionSpec as P

SEQS = 16
HEADS = 32
LANES = 128
CHIP_FEATURES = 4
HALF = 8192


def spread_table():
    table = np.zeros((CHIP_FEATURES, 4, HEADS, LANES), np.float32)
    for i in range(CHIP_FEATURES):
        for h in range(HEADS):
            table[i, :, h, (i // 2) * 64 + h * 2 + i % 2] = 1.0
    return table.reshape(4 * LANES, LANES)


def repeat_table():
    table = np.zeros((4, 4, 4, 16), np.float32)
    for i in range(4):
        for k in range(4):
            table[i, k, :, i * 4 + k] = 1.0
    return table.reshape(64, 16)


def merge_project_kernel(got_ref, weight_ref, spread_ref, repeat_ref, out_ref):
    got = got_ref[...].astype(jnp.float32).reshape(64, 24, LANES)
    stats = got[:, 16:24]
    swapped = pltpu.roll(stats, 4, 1)
    upper = lax.broadcasted_iota(jnp.int32, stats.shape, 1) < 4
    coarse = jnp.where(upper, stats, swapped)
    fine = jnp.where(upper, swapped, stats)
    scale = jnp.exp(coarse - jnp.max(coarse, axis=0, keepdims=True))
    total = jnp.sum(scale * fine, axis=0)
    first = jnp.sum(scale * got[:, 0:8], axis=0) / total
    second = jnp.sum(scale * got[:, 8:16], axis=0) / total
    merged = jnp.concatenate([first, second], axis=0).astype(jnp.bfloat16)
    rows = jnp.dot(repeat_ref[...], merged, preferred_element_type=jnp.float32)
    lane_group = lax.broadcasted_iota(jnp.int32, rows.shape, 1) // 32
    row_group = lax.broadcasted_iota(jnp.int32, rows.shape, 0) % 4
    rows = jnp.where(lane_group == row_group, rows, 0.0).astype(jnp.bfloat16)
    wide = jnp.concatenate([rows[16 * i : 16 * i + 16] for i in range(4)], axis=1)
    left = jnp.dot(wide, spread_ref[...], preferred_element_type=jnp.float32).astype(jnp.bfloat16)
    low = lax.broadcasted_iota(jnp.int32, (8, LANES), 1) < 64
    step = 1024
    for start in range(0, HALF, step):
        part = jnp.dot(
            left, weight_ref[:, start : start + step], preferred_element_type=jnp.float32
        )
        for tile in range(step // LANES):
            piece = part[:, tile * LANES : (tile + 1) * LANES]
            top, bottom = piece[0:8], piece[8:16]
            even = jnp.where(low, top, pltpu.roll(bottom, 64, 1))
            odd = jnp.where(low, pltpu.roll(top, 64, 1), bottom)
            out_ref[start // LANES + tile] = jnp.concatenate([even, odd], axis=0).astype(
                jnp.bfloat16
            )


def merge_project(got, weight):
    vmem = pl.BlockSpec(memory_space=pltpu.VMEM)
    return pl.pallas_call(
        merge_project_kernel,
        out_shape=jax.ShapeDtypeStruct((HALF // LANES, 16, LANES), jnp.bfloat16),
        in_specs=[vmem] * 4,
        out_specs=vmem,
        compiler_params=pltpu.CompilerParams(vmem_limit_bytes=24 * 1024 * 1024),
        cost_estimate=pl.CostEstimate(flops=34_000_000, bytes_accessed=3_000_000, transcendentals=65536),
    )(
        got,
        weight,
        jnp.asarray(spread_table(), jnp.bfloat16),
        jnp.asarray(repeat_table(), jnp.bfloat16),
    )


def final_sum_kernel(got_ref, out_ref):
    total = jnp.sum(got_ref[...].astype(jnp.float32), axis=0)
    total = total[0:8] + total[8:16]
    out_ref[...] = jnp.concatenate([total[:, 0:64], total[:, 64:128]], axis=0).astype(jnp.bfloat16)


def final_sum(got):
    vmem = pl.BlockSpec(memory_space=pltpu.VMEM)
    return pl.pallas_call(
        final_sum_kernel,
        out_shape=jax.ShapeDtypeStruct((SEQS, 64), jnp.bfloat16),
        in_specs=[vmem],
        out_specs=vmem,
        compiler_params=pltpu.CompilerParams(vmem_limit_bytes=16 * 1024 * 1024),
        cost_estimate=pl.CostEstimate(flops=131072, bytes_accessed=264192, transcendentals=0),
    )(got)


def attend(query, key_cache, value_cache, lengths, block_index):
    batch, local_heads, head_size = query.shape
    positions_dev = key_cache.shape[1]
    local_kv = key_cache.shape[2]
    group = local_heads // local_kv
    positions = block_index * positions_dev + jnp.arange(positions_dev, dtype=jnp.int32)
    live = (positions[None, :] < lengths[:, None])[:, None, None, :]
    grouped = query.reshape(batch, local_kv, group, head_size)
    scores = jnp.einsum("bgqd,bpgd->bgqp", grouped, key_cache, preferred_element_type=jnp.float32)
    scores = scores * jnp.float32(head_size**-0.5)
    masked = jnp.where(live, scores, jnp.float32(-1e30))
    block_max = jnp.max(masked, axis=-1)
    weights = jnp.where(live, jnp.exp(scores - block_max[..., None]), jnp.float32(0.0))
    block_total = jnp.sum(weights, axis=-1)
    summed = jnp.einsum(
        "bgqp,bpgd->bgqd",
        weights.astype(jnp.bfloat16),
        value_cache,
        preferred_element_type=jnp.float32,
    )
    floored = jnp.maximum(block_total, jnp.float32(1.0))
    coarse = lax.reduce_precision(block_max + jnp.log(floored), 8, 7)
    some = block_total > 0
    fine = jnp.where(some, floored * jnp.exp(jnp.where(some, block_max - coarse, 0.0)), 0.0)
    fine = lax.reduce_precision(fine, 8, 7)
    scaled = (summed * (fine / floored)[..., None]).astype(jnp.bfloat16)
    features = scaled.reshape(batch * local_heads, head_size).T.reshape(32, 16, LANES)
    stats = jnp.concatenate([coarse.reshape(4, LANES), fine.reshape(4, LANES)]).astype(jnp.bfloat16)
    stats = jnp.broadcast_to(stats[None], (32, 8, LANES))
    return jnp.concatenate([features, stats], axis=1)


def local(query, key_cache, value_cache, lengths, out_weight):
    core = lax.axis_index("core")
    block_index = lax.axis_index("chip") * 2 + core
    packed = attend(query, key_cache, value_cache, lengths, block_index)
    packed = jnp.broadcast_to(packed[:, None], (32, 2, 24, LANES)).reshape(64, 24, LANES)
    got = lax.all_to_all(packed, ("chip", "core"), split_axis=0, concat_axis=0, tiled=True)

    halves = out_weight.reshape(HEADS, 2, 32, 2, 256)
    mine = lax.dynamic_index_in_dim(halves, core, axis=3, keepdims=False).reshape(64, HALF)
    theirs = lax.dynamic_index_in_dim(halves, 1 - core, axis=3, keepdims=False).reshape(64, HALF)
    arrived = lax.ppermute(theirs, "core", [(0, 1), (1, 0)])
    weight = jnp.concatenate(
        [jnp.where(core == 0, mine, arrived), jnp.where(core == 0, arrived, mine)]
    )

    terms = merge_project(got.reshape(32, 48, LANES), weight)
    terms = lax.all_to_all(
        terms.reshape(128, 8, LANES), ("chip", "tp"), split_axis=0, concat_axis=0, tiled=True
    )
    return final_sum(terms.reshape(64, 16, LANES))


def solution(mesh):
    parts = Mesh(mesh.devices.reshape(32, 2, 4), ("chip", "core", "tp"))
    placed = (
        P(None, "tp", None),
        P(None, ("chip", "core"), "tp", None),
        P(None, ("chip", "core"), "tp", None),
        P(),
        P("tp", ("chip", "core"), None),
    )
    return jax.shard_map(
        local,
        mesh=parts,
        in_specs=placed,
        out_specs=P(None, ("chip", "core", "tp")),
        check_vma=False,
    )
```

```python
import functools

import jax
import jax.numpy as jnp
import numpy as np
from jax import lax
from jax.experimental import pallas as pl
from jax.experimental.pallas import tpu as pltpu
from jax.sharding import Mesh
from jax.sharding import PartitionSpec as P

SEQS = 16
HEADS = 32
LANES = 128
CHIP_FEATURES = 4
HALF = 8192
PER = 4
GROUPS = SEQS // PER


def spread_table():
    table = np.zeros((CHIP_FEATURES, 4, HEADS, LANES), np.float32)
    for i in range(CHIP_FEATURES):
        for h in range(HEADS):
            table[i, :, h, (i // 2) * 64 + h * 2 + i % 2] = 1.0
    return table.reshape(4 * LANES, LANES)


def repeat_table():
    table = np.zeros((4, 4, 4, 16), np.float32)
    for i in range(4):
        for k in range(4):
            table[i, k, :, i * 4 + k] = 1.0
    return table.reshape(64, 16)


def merge_project_kernel(got_ref, weight_ref, spread_ref, repeat_ref, out_ref):
    got = got_ref[...].astype(jnp.float32).reshape(64, 24, LANES)
    stats = got[:, 16:24]
    swapped = pltpu.roll(stats, 4, 1)
    upper = lax.broadcasted_iota(jnp.int32, stats.shape, 1) < 4
    coarse = jnp.where(upper, stats, swapped)
    fine = jnp.where(upper, swapped, stats)
    scale = jnp.exp(coarse - jnp.max(coarse, axis=0, keepdims=True))
    total = jnp.sum(scale * fine, axis=0)
    first = jnp.sum(scale * got[:, 0:8], axis=0) / total
    second = jnp.sum(scale * got[:, 8:16], axis=0) / total
    merged = jnp.concatenate([first, second], axis=0).astype(jnp.bfloat16)
    rows = jnp.dot(repeat_ref[...], merged, preferred_element_type=jnp.float32)
    lane_group = lax.broadcasted_iota(jnp.int32, rows.shape, 1) // 32
    row_group = lax.broadcasted_iota(jnp.int32, rows.shape, 0) % 4
    rows = jnp.where(lane_group == row_group, rows, 0.0).astype(jnp.bfloat16)
    wide = jnp.concatenate([rows[16 * i : 16 * i + 16] for i in range(4)], axis=1)
    left = jnp.dot(wide, spread_ref[...], preferred_element_type=jnp.float32).astype(jnp.bfloat16)
    low = lax.broadcasted_iota(jnp.int32, (8, LANES), 1) < 64
    step = 1024
    for start in range(0, HALF, step):
        part = jnp.dot(
            left, weight_ref[:, start : start + step], preferred_element_type=jnp.float32
        )
        for tile in range(step // LANES):
            piece = part[:, tile * LANES : (tile + 1) * LANES]
            top, bottom = piece[0:8], piece[8:16]
            even = jnp.where(low, top, pltpu.roll(bottom, 64, 1))
            odd = jnp.where(low, pltpu.roll(top, 64, 1), bottom)
            out_ref[start // LANES + tile] = jnp.concatenate([even, odd], axis=0).astype(
                jnp.bfloat16
            )


def merge_project(got, weight):
    vmem = pl.BlockSpec(memory_space=pltpu.VMEM)
    return pl.pallas_call(
        merge_project_kernel,
        out_shape=jax.ShapeDtypeStruct((HALF // LANES, 16, LANES), jnp.bfloat16),
        in_specs=[vmem] * 4,
        out_specs=vmem,
        compiler_params=pltpu.CompilerParams(vmem_limit_bytes=24 * 1024 * 1024),
        cost_estimate=pl.CostEstimate(flops=34_000_000, bytes_accessed=3_000_000, transcendentals=65536),
    )(
        got,
        weight,
        jnp.asarray(spread_table(), jnp.bfloat16),
        jnp.asarray(repeat_table(), jnp.bfloat16),
    )


def final_sum_kernel(got_ref, out_ref):
    total = jnp.sum(got_ref[...].astype(jnp.float32), axis=0)
    total = total[0:8] + total[8:16]
    out_ref[...] = jnp.concatenate([total[:, 0:64], total[:, 64:128]], axis=0).astype(jnp.bfloat16)


def final_sum(got):
    vmem = pl.BlockSpec(memory_space=pltpu.VMEM)
    return pl.pallas_call(
        final_sum_kernel,
        out_shape=jax.ShapeDtypeStruct((SEQS, 64), jnp.bfloat16),
        in_specs=[vmem],
        out_specs=vmem,
        compiler_params=pltpu.CompilerParams(vmem_limit_bytes=16 * 1024 * 1024),
        cost_estimate=pl.CostEstimate(flops=131072, bytes_accessed=264192, transcendentals=0),
    )(got)


def attend_kernel(
    lengths_hbm,
    query_hbm,
    key_hbm,
    value_hbm,
    out_ref,
    lengths_ref,
    query_ref,
    keys,
    values,
    outs,
    turned,
    small_sem,
    key_sem,
    value_sem,
):
    width = key_hbm.shape[1]
    block_index = lax.axis_index("chip") * 2 + lax.axis_index("core")
    base = block_index * (width // 2)
    query_copy = pltpu.make_async_copy(query_hbm, query_ref, small_sem.at[0])
    lengths_copy = pltpu.make_async_copy(lengths_hbm, lengths_ref, small_sem.at[1])
    key_copies = []
    value_copies = []
    for b in range(SEQS):
        key_copies.append(pltpu.make_async_copy(key_hbm.at[b], keys.at[b], key_sem.at[b]))
        value_copies.append(pltpu.make_async_copy(value_hbm.at[b], values.at[b], value_sem.at[b]))
    query_copy.start()
    lengths_copy.start()
    for t in range(GROUPS + 1):
        if t < GROUPS:
            for b in range(PER * t, PER * t + PER):
                key_copies[b].start()
        if t > 0:
            for b in range(PER * t - PER, PER * t):
                value_copies[b].start()

    column = lax.broadcasted_iota(jnp.int32, (HEADS, width), 1)
    row = lax.broadcasted_iota(jnp.int32, (HEADS, width), 0)
    position = jnp.where((column % 2) == (row // 16), column // 2, jnp.int32(1 << 30))
    lane = lax.broadcasted_iota(jnp.int32, (HEADS, LANES), 1)
    factor = jnp.float32(LANES**-0.5)
    query_copy.wait()
    lengths_copy.wait()
    scores, weights, tops, totals, stats = {}, {}, {}, {}, [0.0] * 4
    for t in range(GROUPS + 2):
        first = range(PER * t, PER * t + PER) if t < GROUPS else ()
        second = range(PER * (t - 1), PER * t) if 1 <= t <= GROUPS else ()
        third = range(PER * (t - 2), PER * (t - 1)) if t >= 2 else ()
        for b in first:
            key_copies[b].wait()
        for b in third:
            value_copies[b].wait()
        for b in first:
            raw = lax.dot_general(
                query_ref[b],
                keys[b],
                (((1,), (1,)), ((), ())),
                preferred_element_type=jnp.float32,
            )
            scores[b] = jnp.where(position < lengths_ref[b] - base, raw, jnp.float32(-1e30))
        for b in second:
            top = jnp.max(scores[b], axis=1, keepdims=True)
            weight = jnp.exp((scores[b] - top) * factor)
            totals[b] = jnp.sum(weight, axis=1, keepdims=True)
            tops[b] = top * factor
            weights[b] = weight.astype(jnp.bfloat16)
        for b in third:
            summed = jnp.dot(weights[b], values[b], preferred_element_type=jnp.float32)
            coarse = (tops[b] + jnp.log(totals[b])).astype(jnp.bfloat16).astype(jnp.float32)
            fine = totals[b] * jnp.exp(tops[b] - coarse)
            fine = fine.astype(jnp.bfloat16).astype(jnp.float32)
            fine = jnp.where(lengths_ref[b] > base, fine, 0.0)
            outs[b * HEADS : b * HEADS + HEADS] = summed * (fine / totals[b])
            k = b // 4
            stats[b % 4] = jnp.where(
                lane == k, coarse, jnp.where(lane == k + 4, fine, stats[b % 4])
            )
            if b % 4 == 3:
                turned[pl.ds(k, LANES, stride=4), :] = outs[k * LANES : k * LANES + LANES].T
    packed = jnp.concatenate(stats, axis=0).T[0:8]
    features = turned[...].reshape(32, 16, LANES)
    packed = jnp.broadcast_to(packed[None], (32, 8, LANES))
    out_ref[...] = jnp.concatenate([features, packed, features, packed], axis=1).astype(
        jnp.bfloat16
    )


def attend(query, key_cache, value_cache, lengths):
    width = key_cache.shape[1] * key_cache.shape[2]
    keys = key_cache.reshape(SEQS, width, LANES)
    values = value_cache.reshape(SEQS, width, LANES)
    vmem = pl.BlockSpec(memory_space=pltpu.VMEM)
    hbm = pl.BlockSpec(memory_space=pltpu.HBM)
    return pl.pallas_call(
        attend_kernel,
        out_shape=jax.ShapeDtypeStruct((32, 48, LANES), jnp.bfloat16),
        in_specs=[hbm] * 4,
        out_specs=vmem,
        scratch_shapes=[
            pltpu.SMEM((SEQS,), jnp.int32),
            pltpu.VMEM((SEQS, HEADS, LANES), jnp.bfloat16),
            pltpu.VMEM((SEQS, width, LANES), jnp.bfloat16),
            pltpu.VMEM((SEQS, width, LANES), jnp.bfloat16),
            pltpu.VMEM((512, LANES), jnp.float32),
            pltpu.VMEM((512, LANES), jnp.float32),
            pltpu.SemaphoreType.DMA((2,)),
            pltpu.SemaphoreType.DMA((SEQS,)),
            pltpu.SemaphoreType.DMA((SEQS,)),
        ],
        compiler_params=pltpu.CompilerParams(vmem_limit_bytes=60 * 1024 * 1024),
        cost_estimate=pl.CostEstimate(
            flops=270_000_000, bytes_accessed=8_800_000, transcendentals=540_000
        ),
    )(lengths, query, keys, values)


def split_kernel(own_ref, other_ref, out_ref):
    core = lax.axis_index("core")
    for t in range(own_ref.shape[2] // 512):
        start = pl.multiple_of(t * 512 + core * 256, 256)
        for which, ref in ((core, own_ref), (1 - core, other_ref)):
            rows = pl.ds(pl.multiple_of(which * 64, 64), 64)
            piece = ref[:, :, pl.ds(start, 256)]
            out_ref[rows, t * 256 : (t + 1) * 256] = piece.reshape(64, 256)


def split_weight(own, other):
    vmem = pl.BlockSpec(memory_space=pltpu.VMEM)
    return pl.pallas_call(
        split_kernel,
        out_shape=jax.ShapeDtypeStruct((LANES, HALF), jnp.bfloat16),
        in_specs=[vmem, vmem],
        out_specs=vmem,
        compiler_params=pltpu.CompilerParams(vmem_limit_bytes=16 * 1024 * 1024),
        cost_estimate=pl.CostEstimate(flops=0, bytes_accessed=4_194_304, transcendentals=0),
    )(own, other)


def local(query, key_cache, value_cache, lengths, out_weight):
    packed = attend(query, key_cache, value_cache, lengths)
    packed, out_weight = lax.optimization_barrier((packed, out_weight))
    got = lax.all_to_all(
        packed.reshape(64, 24, LANES), ("chip", "core"), split_axis=0, concat_axis=0, tiled=True
    )
    other = lax.ppermute(out_weight, "core", [(0, 1), (1, 0)])
    weight = split_weight(out_weight, other)

    terms = merge_project(got.reshape(32, 48, LANES), weight)
    terms = lax.all_to_all(
        terms.reshape(128, 8, LANES), ("chip", "tp"), split_axis=0, concat_axis=0, tiled=True
    )
    return final_sum(terms.reshape(64, 16, LANES))


def solution(mesh):
    parts = Mesh(mesh.devices.reshape(32, 2, 4), ("chip", "core", "tp"))
    placed = (
        P(None, "tp", None),
        P(None, ("chip", "core"), "tp", None),
        P(None, ("chip", "core"), "tp", None),
        P(),
        P("tp", ("chip", "core"), None),
    )
    return jax.shard_map(
        local,
        mesh=parts,
        in_specs=placed,
        out_specs=P(None, ("chip", "core", "tp")),
        check_vma=False,
    )
```

```python
import functools

import jax
import jax.numpy as jnp
import numpy as np
from jax import lax
from jax.experimental import pallas as pl
from jax.experimental.pallas import tpu as pltpu
from jax.sharding import Mesh
from jax.sharding import PartitionSpec as P

SEQS = 16
HEADS = 32
LANES = 128
CHIP_FEATURES = 4
HALF = 8192
PER = 4
AHEAD = 4
GROUPS = SEQS // PER


def spread_table():
    table = np.zeros((CHIP_FEATURES, 4, HEADS, LANES), np.float32)
    for i in range(CHIP_FEATURES):
        for h in range(HEADS):
            table[i, :, h, (i // 2) * 64 + h * 2 + i % 2] = 1.0
    return table.reshape(4 * LANES, LANES)


def repeat_table():
    table = np.zeros((4, 4, 4, 16), np.float32)
    for i in range(4):
        for k in range(4):
            table[i, k, :, i * 4 + k] = 1.0
    return table.reshape(64, 16)


def merge_kernel(got_ref, out_ref):
    got = got_ref[...].astype(jnp.float32).reshape(32, 24, LANES)
    stats = got[:, 16:24]
    swapped = pltpu.roll(stats, 4, 1)
    upper = lax.broadcasted_iota(jnp.int32, stats.shape, 1) < 4
    coarse = jnp.where(upper, stats, swapped)
    fine = jnp.where(upper, swapped, stats)
    highest = jnp.max(coarse, axis=0)
    scale = jnp.exp(coarse - highest[None])
    out_ref[0:8] = jnp.sum(scale * got[:, 0:8], axis=0)
    out_ref[8:16] = jnp.sum(scale * got[:, 8:16], axis=0)
    out_ref[16:24] = highest
    out_ref[24:32] = jnp.sum(scale * fine, axis=0)


def merge(got):
    vmem = pl.BlockSpec(memory_space=pltpu.VMEM)
    return pl.pallas_call(
        merge_kernel,
        out_shape=jax.ShapeDtypeStruct((32, LANES), jnp.float32),
        in_specs=[vmem],
        out_specs=vmem,
        compiler_params=pltpu.CompilerParams(vmem_limit_bytes=16 * 1024 * 1024),
        cost_estimate=pl.CostEstimate(flops=400_000, bytes_accessed=212_992, transcendentals=32768),
    )(got)


def project_kernel(own_ref, other_ref, weight_ref, spread_ref, repeat_ref, out_ref):
    highest = jnp.maximum(own_ref[16:24], other_ref[16:24])
    own_scale = jnp.exp(own_ref[16:24] - highest)
    other_scale = jnp.exp(other_ref[16:24] - highest)
    total = own_scale * own_ref[24:32] + other_scale * other_ref[24:32]
    first = (own_scale * own_ref[0:8] + other_scale * other_ref[0:8]) / total
    second = (own_scale * own_ref[8:16] + other_scale * other_ref[8:16]) / total
    merged = jnp.concatenate([first, second], axis=0).astype(jnp.bfloat16)
    rows = jnp.dot(repeat_ref[...], merged, preferred_element_type=jnp.float32)
    lane_group = lax.broadcasted_iota(jnp.int32, rows.shape, 1) // 32
    row_group = lax.broadcasted_iota(jnp.int32, rows.shape, 0) % 4
    rows = jnp.where(lane_group == row_group, rows, 0.0).astype(jnp.bfloat16)
    wide = jnp.concatenate([rows[16 * i : 16 * i + 16] for i in range(4)], axis=1)
    left = jnp.dot(wide, spread_ref[...], preferred_element_type=jnp.float32).astype(jnp.bfloat16)
    low = lax.broadcasted_iota(jnp.int32, (8, LANES), 1) < 64
    step = 1024
    for start in range(0, HALF, step):
        part = jnp.dot(
            left, weight_ref[:, start : start + step], preferred_element_type=jnp.float32
        )
        for tile in range(step // LANES):
            piece = part[:, tile * LANES : (tile + 1) * LANES]
            top, bottom = piece[0:8], piece[8:16]
            even = jnp.where(low, top, pltpu.roll(bottom, 64, 1))
            odd = jnp.where(low, pltpu.roll(top, 64, 1), bottom)
            out_ref[start // LANES + tile] = jnp.concatenate([even, odd], axis=0).astype(
                jnp.bfloat16
            )


def project(own, other, weight):
    vmem = pl.BlockSpec(memory_space=pltpu.VMEM)
    return pl.pallas_call(
        project_kernel,
        out_shape=jax.ShapeDtypeStruct((HALF // LANES, 16, LANES), jnp.bfloat16),
        in_specs=[vmem] * 5,
        out_specs=vmem,
        compiler_params=pltpu.CompilerParams(vmem_limit_bytes=24 * 1024 * 1024),
        cost_estimate=pl.CostEstimate(flops=34_000_000, bytes_accessed=3_000_000, transcendentals=65536),
    )(
        own,
        other,
        weight,
        jnp.asarray(spread_table(), jnp.bfloat16),
        jnp.asarray(repeat_table(), jnp.bfloat16),
    )


def final_sum_kernel(got_ref, out_ref):
    total = jnp.sum(got_ref[...].astype(jnp.float32), axis=0)
    total = total[0:8] + total[8:16]
    out_ref[...] = jnp.concatenate([total[:, 0:64], total[:, 64:128]], axis=0).astype(jnp.bfloat16)


def final_sum(got):
    vmem = pl.BlockSpec(memory_space=pltpu.VMEM)
    return pl.pallas_call(
        final_sum_kernel,
        out_shape=jax.ShapeDtypeStruct((SEQS, 64), jnp.bfloat16),
        in_specs=[vmem],
        out_specs=vmem,
        compiler_params=pltpu.CompilerParams(vmem_limit_bytes=16 * 1024 * 1024),
        cost_estimate=pl.CostEstimate(flops=131072, bytes_accessed=264192, transcendentals=0),
    )(got)


def attend_kernel(
    lengths_hbm,
    query_hbm,
    key_hbm,
    value_hbm,
    out_ref,
    lengths_ref,
    query_ref,
    keys,
    values,
    outs,
    turned,
    small_sem,
    key_sem,
    value_sem,
):
    width = key_hbm.shape[1]
    block_index = lax.axis_index("chip") * 2 + lax.axis_index("core")
    base = block_index * (width // 2)
    query_copy = pltpu.make_async_copy(query_hbm, query_ref, small_sem.at[0])
    lengths_copy = pltpu.make_async_copy(lengths_hbm, lengths_ref, small_sem.at[1])
    key_copies = []
    value_copies = []
    for b in range(SEQS):
        key_copies.append(pltpu.make_async_copy(key_hbm.at[b], keys.at[b], key_sem.at[b]))
        value_copies.append(pltpu.make_async_copy(value_hbm.at[b], values.at[b], value_sem.at[b]))
    query_copy.start()
    lengths_copy.start()
    loads = []
    for t in range(GROUPS + 1):
        if t < GROUPS:
            loads.append(key_copies[PER * t : PER * t + PER])
        if t > 0:
            loads.append(value_copies[PER * t - PER : PER * t])
    for copy in sum(loads[:AHEAD], []):
        copy.start()
    begun, used = AHEAD, 0

    column = lax.broadcasted_iota(jnp.int32, (HEADS, width), 1)
    row = lax.broadcasted_iota(jnp.int32, (HEADS, width), 0)
    position = jnp.where((column % 2) == (row // 16), column // 2, jnp.int32(1 << 30))
    lane = lax.broadcasted_iota(jnp.int32, (HEADS, LANES), 1)
    factor = jnp.float32(LANES**-0.5)
    query_copy.wait()
    lengths_copy.wait()
    scores, weights, tops, totals, stats = {}, {}, {}, {}, [0.0] * 4
    for t in range(GROUPS + 2):
        first = range(PER * t, PER * t + PER) if t < GROUPS else ()
        second = range(PER * (t - 1), PER * t) if 1 <= t <= GROUPS else ()
        third = range(PER * (t - 2), PER * (t - 1)) if t >= 2 else ()
        for b in first:
            key_copies[b].wait()
        for b in third:
            value_copies[b].wait()
        used += (len(first) + len(third)) // PER
        for copy in sum(loads[begun : used + AHEAD], []):
            copy.start()
        begun = max(begun, used + AHEAD)
        for b in first:
            raw = lax.dot_general(
                query_ref[b],
                keys[b],
                (((1,), (1,)), ((), ())),
                preferred_element_type=jnp.float32,
            )
            scores[b] = jnp.where(position < lengths_ref[b] - base, raw, jnp.float32(-1e30))
        for b in second:
            top = jnp.max(scores[b], axis=1, keepdims=True)
            weight = jnp.exp((scores[b] - top) * factor)
            totals[b] = jnp.sum(weight, axis=1, keepdims=True)
            tops[b] = top * factor
            weights[b] = weight.astype(jnp.bfloat16)
        for b in third:
            summed = jnp.dot(weights[b], values[b], preferred_element_type=jnp.float32)
            coarse = (tops[b] + jnp.log(totals[b])).astype(jnp.bfloat16).astype(jnp.float32)
            fine = totals[b] * jnp.exp(tops[b] - coarse)
            fine = fine.astype(jnp.bfloat16).astype(jnp.float32)
            fine = jnp.where(lengths_ref[b] > base, fine, 0.0)
            outs[b * HEADS : b * HEADS + HEADS] = summed * (fine / totals[b])
            k = b // 4
            stats[b % 4] = jnp.where(
                lane == k, coarse, jnp.where(lane == k + 4, fine, stats[b % 4])
            )
            if b % 4 == 3:
                turned[pl.ds(k, LANES, stride=4), :] = outs[k * LANES : k * LANES + LANES].T
    packed = jnp.concatenate(stats, axis=0).T[0:8]
    features = turned[...].reshape(16, 2, 16, LANES)
    packed = jnp.broadcast_to(packed[None], (16, 8, LANES))
    out_ref[...] = jnp.concatenate(
        [features[:, 0], packed, features[:, 1], packed], axis=1
    ).astype(jnp.bfloat16)


def attend(query, key_cache, value_cache, lengths):
    width = key_cache.shape[1] * key_cache.shape[2]
    keys = key_cache.reshape(SEQS, width, LANES)
    values = value_cache.reshape(SEQS, width, LANES)
    vmem = pl.BlockSpec(memory_space=pltpu.VMEM)
    hbm = pl.BlockSpec(memory_space=pltpu.HBM)
    return pl.pallas_call(
        attend_kernel,
        out_shape=jax.ShapeDtypeStruct((16, 48, LANES), jnp.bfloat16),
        in_specs=[hbm] * 4,
        out_specs=vmem,
        scratch_shapes=[
            pltpu.SMEM((SEQS,), jnp.int32),
            pltpu.VMEM((SEQS, HEADS, LANES), jnp.bfloat16),
            pltpu.VMEM((SEQS, width, LANES), jnp.bfloat16),
            pltpu.VMEM((SEQS, width, LANES), jnp.bfloat16),
            pltpu.VMEM((512, LANES), jnp.float32),
            pltpu.VMEM((512, LANES), jnp.float32),
            pltpu.SemaphoreType.DMA((2,)),
            pltpu.SemaphoreType.DMA((SEQS,)),
            pltpu.SemaphoreType.DMA((SEQS,)),
        ],
        compiler_params=pltpu.CompilerParams(vmem_limit_bytes=60 * 1024 * 1024),
        cost_estimate=pl.CostEstimate(
            flops=270_000_000, bytes_accessed=8_800_000, transcendentals=540_000
        ),
    )(lengths, query, keys, values)


def split_kernel(own_ref, other_ref, out_ref):
    core = lax.axis_index("core")
    for t in range(own_ref.shape[2] // 512):
        start = pl.multiple_of(t * 512 + core * 256, 256)
        for which, ref in ((core, own_ref), (1 - core, other_ref)):
            rows = pl.ds(pl.multiple_of(which * 64, 64), 64)
            piece = ref[:, :, pl.ds(start, 256)]
            out_ref[rows, t * 256 : (t + 1) * 256] = piece.reshape(64, 256)


def split_weight(own, other):
    vmem = pl.BlockSpec(memory_space=pltpu.VMEM)
    return pl.pallas_call(
        split_kernel,
        out_shape=jax.ShapeDtypeStruct((LANES, HALF), jnp.bfloat16),
        in_specs=[vmem, vmem],
        out_specs=vmem,
        compiler_params=pltpu.CompilerParams(vmem_limit_bytes=16 * 1024 * 1024),
        cost_estimate=pl.CostEstimate(flops=0, bytes_accessed=4_194_304, transcendentals=0),
    )(own, other)


def local(query, key_cache, value_cache, lengths, out_weight):
    packed = attend(query, key_cache, value_cache, lengths)
    packed, out_weight = lax.optimization_barrier((packed, out_weight))
    got = lax.all_to_all(
        packed.reshape(32, 24, LANES), "chip", split_axis=0, concat_axis=0, tiled=True
    )
    other = lax.ppermute(out_weight, "core", [(0, 1), (1, 0)])
    weight = split_weight(out_weight, other)

    part = merge(got.reshape(16, 48, LANES))
    other_part = lax.ppermute(part, "core", [(0, 1), (1, 0)])
    terms = project(part, other_part, weight)
    terms = lax.all_to_all(
        terms.reshape(128, 8, LANES), ("chip", "tp"), split_axis=0, concat_axis=0, tiled=True
    )
    return final_sum(terms.reshape(64, 16, LANES))


def solution(mesh):
    parts = Mesh(mesh.devices.reshape(32, 2, 4), ("chip", "core", "tp"))
    placed = (
        P(None, "tp", None),
        P(None, ("chip", "core"), "tp", None),
        P(None, ("chip", "core"), "tp", None),
        P(),
        P("tp", ("chip", "core"), None),
    )
    return jax.shard_map(
        local,
        mesh=parts,
        in_specs=placed,
        out_specs=P(None, ("chip", "core", "tp")),
        check_vma=False,
    )
```

```python
import functools

import jax
import jax.numpy as jnp
import numpy as np
from jax import lax
from jax.experimental import pallas as pl
from jax.experimental.pallas import tpu as pltpu
from jax.sharding import Mesh
from jax.sharding import PartitionSpec as P

SEQS = 16
HEADS = 32
LANES = 128
CHIP_FEATURES = 4
HALF = 8192
PER = 4
AHEAD = 4
GROUPS = SEQS // PER


def spread_table():
    table = np.zeros((CHIP_FEATURES, 4, HEADS, LANES), np.float32)
    for i in range(CHIP_FEATURES):
        for h in range(HEADS):
            table[i, :, h, (i // 2) * 64 + h * 2 + i % 2] = 1.0
    return table.reshape(4 * LANES, LANES)


def repeat_table():
    table = np.zeros((4, 4, 4, 16), np.float32)
    for i in range(4):
        for k in range(4):
            table[i, k, :, i * 4 + k] = 1.0
    return table.reshape(64, 16)


def merge_kernel(got_ref, out_ref):
    got = got_ref[...].astype(jnp.float32).reshape(32, 24, LANES)
    stats = got[:, 16:24]
    swapped = pltpu.roll(stats, 4, 1)
    upper = lax.broadcasted_iota(jnp.int32, stats.shape, 1) < 4
    coarse = jnp.where(upper, stats, swapped)
    fine = jnp.where(upper, swapped, stats)
    highest = jnp.max(coarse, axis=0)
    scale = jnp.exp(coarse - highest[None])
    out_ref[0:8] = jnp.sum(scale * got[:, 0:8], axis=0)
    out_ref[8:16] = jnp.sum(scale * got[:, 8:16], axis=0)
    out_ref[16:24] = highest
    out_ref[24:32] = jnp.sum(scale * fine, axis=0)


def merge(got):
    vmem = pl.BlockSpec(memory_space=pltpu.VMEM)
    return pl.pallas_call(
        merge_kernel,
        out_shape=jax.ShapeDtypeStruct((32, LANES), jnp.float32),
        in_specs=[vmem],
        out_specs=vmem,
        compiler_params=pltpu.CompilerParams(vmem_limit_bytes=16 * 1024 * 1024),
        cost_estimate=pl.CostEstimate(flops=400_000, bytes_accessed=212_992, transcendentals=32768),
    )(got)


def project_kernel(own_ref, other_ref, weight_ref, spread_ref, repeat_ref, out_ref):
    highest = jnp.maximum(own_ref[16:24], other_ref[16:24])
    own_scale = jnp.exp(own_ref[16:24] - highest)
    other_scale = jnp.exp(other_ref[16:24] - highest)
    total = own_scale * own_ref[24:32] + other_scale * other_ref[24:32]
    first = (own_scale * own_ref[0:8] + other_scale * other_ref[0:8]) / total
    second = (own_scale * own_ref[8:16] + other_scale * other_ref[8:16]) / total
    merged = jnp.concatenate([first, second], axis=0).astype(jnp.bfloat16)
    rows = jnp.dot(repeat_ref[...], merged, preferred_element_type=jnp.float32)
    lane_group = lax.broadcasted_iota(jnp.int32, rows.shape, 1) // 32
    row_group = lax.broadcasted_iota(jnp.int32, rows.shape, 0) % 4
    rows = jnp.where(lane_group == row_group, rows, 0.0).astype(jnp.bfloat16)
    wide = jnp.concatenate([rows[16 * i : 16 * i + 16] for i in range(4)], axis=1)
    left = jnp.dot(wide, spread_ref[...], preferred_element_type=jnp.float32).astype(jnp.bfloat16)
    low = lax.broadcasted_iota(jnp.int32, (8, LANES), 1) < 64
    step = 1024
    for start in range(0, HALF, step):
        part = jnp.dot(
            left, weight_ref[:, start : start + step], preferred_element_type=jnp.float32
        )
        for tile in range(step // LANES):
            piece = part[:, tile * LANES : (tile + 1) * LANES]
            top, bottom = piece[0:8], piece[8:16]
            even = jnp.where(low, top, pltpu.roll(bottom, 64, 1))
            odd = jnp.where(low, pltpu.roll(top, 64, 1), bottom)
            out_ref[start // LANES + tile] = jnp.concatenate([even, odd], axis=0).astype(
                jnp.bfloat16
            )


def project(own, other, weight):
    vmem = pl.BlockSpec(memory_space=pltpu.VMEM)
    return pl.pallas_call(
        project_kernel,
        out_shape=jax.ShapeDtypeStruct((HALF // LANES, 16, LANES), jnp.bfloat16),
        in_specs=[vmem] * 5,
        out_specs=vmem,
        compiler_params=pltpu.CompilerParams(vmem_limit_bytes=24 * 1024 * 1024),
        cost_estimate=pl.CostEstimate(flops=34_000_000, bytes_accessed=3_000_000, transcendentals=65536),
    )(
        own,
        other,
        weight,
        jnp.asarray(spread_table(), jnp.bfloat16),
        jnp.asarray(repeat_table(), jnp.bfloat16),
    )


def final_sum_kernel(got_ref, out_ref):
    total = jnp.sum(got_ref[...].astype(jnp.float32), axis=0)
    total = total[0:8] + total[8:16]
    out_ref[...] = jnp.concatenate([total[:, 0:64], total[:, 64:128]], axis=0).astype(jnp.bfloat16)


def final_sum(got):
    vmem = pl.BlockSpec(memory_space=pltpu.VMEM)
    return pl.pallas_call(
        final_sum_kernel,
        out_shape=jax.ShapeDtypeStruct((SEQS, 64), jnp.bfloat16),
        in_specs=[vmem],
        out_specs=vmem,
        compiler_params=pltpu.CompilerParams(vmem_limit_bytes=16 * 1024 * 1024),
        cost_estimate=pl.CostEstimate(flops=131072, bytes_accessed=264192, transcendentals=0),
    )(got)


def attend_kernel(
    lengths_hbm,
    query_hbm,
    key_hbm,
    value_hbm,
    out_ref,
    lengths_ref,
    query_ref,
    keys,
    values,
    outs,
    turned,
    small_sem,
    key_sem,
    value_sem,
):
    width = key_hbm.shape[1]
    block_index = lax.axis_index("chip") * 2 + lax.axis_index("core")
    base = block_index * (width // 2)
    query_copy = pltpu.make_async_copy(query_hbm, query_ref, small_sem.at[0])
    lengths_copy = pltpu.make_async_copy(lengths_hbm, lengths_ref, small_sem.at[1])
    key_copies = []
    value_copies = []
    for t in range(GROUPS):
        rows = pl.ds(PER * t, PER)
        key_copies.append(pltpu.make_async_copy(key_hbm.at[rows], keys.at[rows], key_sem.at[t]))
        value_copies.append(
            pltpu.make_async_copy(value_hbm.at[rows], values.at[rows], value_sem.at[t])
        )
    query_copy.start()
    lengths_copy.start()
    loads = []
    for t in range(GROUPS + 1):
        if t < GROUPS:
            loads.append(key_copies[t])
        if t > 0:
            loads.append(value_copies[t - 1])
    for copy in loads[:AHEAD]:
        copy.start()
    begun, used = AHEAD, 0

    column = lax.broadcasted_iota(jnp.int32, (HEADS, width), 1)
    row = lax.broadcasted_iota(jnp.int32, (HEADS, width), 0)
    position = jnp.where((column % 2) == (row // 16), column // 2, jnp.int32(1 << 30))
    lane = lax.broadcasted_iota(jnp.int32, (HEADS, LANES), 1)
    factor = jnp.float32(LANES**-0.5)
    query_copy.wait()
    lengths_copy.wait()
    scores, weights, tops, totals, stats = {}, {}, {}, {}, [0.0] * 4
    for t in range(GROUPS + 2):
        first = range(PER * t, PER * t + PER) if t < GROUPS else ()
        second = range(PER * (t - 1), PER * t) if 1 <= t <= GROUPS else ()
        third = range(PER * (t - 2), PER * (t - 1)) if t >= 2 else ()
        if first:
            key_copies[t].wait()
        if third:
            value_copies[t - 2].wait()
        used += (len(first) + len(third)) // PER
        for copy in loads[begun : used + AHEAD]:
            copy.start()
        begun = max(begun, used + AHEAD)
        for b in first:
            raw = lax.dot_general(
                query_ref[b],
                keys[b],
                (((1,), (1,)), ((), ())),
                preferred_element_type=jnp.float32,
            )
            scores[b] = jnp.where(position < lengths_ref[b] - base, raw, jnp.float32(-1e30))
        for b in second:
            top = jnp.max(scores[b], axis=1, keepdims=True)
            weight = jnp.exp((scores[b] - top) * factor)
            totals[b] = jnp.sum(weight, axis=1, keepdims=True)
            tops[b] = top * factor
            weights[b] = weight.astype(jnp.bfloat16)
        for b in third:
            summed = jnp.dot(weights[b], values[b], preferred_element_type=jnp.float32)
            coarse = (tops[b] + jnp.log(totals[b])).astype(jnp.bfloat16).astype(jnp.float32)
            fine = totals[b] * jnp.exp(tops[b] - coarse)
            fine = fine.astype(jnp.bfloat16).astype(jnp.float32)
            fine = jnp.where(lengths_ref[b] > base, fine, 0.0)
            outs[b * HEADS : b * HEADS + HEADS] = summed * (fine / totals[b])
            k = b // 4
            stats[b % 4] = jnp.where(
                lane == k, coarse, jnp.where(lane == k + 4, fine, stats[b % 4])
            )
            if b % 4 == 3:
                turned[pl.ds(k, LANES, stride=4), :] = outs[k * LANES : k * LANES + LANES].T
    packed = jnp.concatenate(stats, axis=0).T[0:8]
    features = turned[...].reshape(16, 2, 16, LANES)
    packed = jnp.broadcast_to(packed[None], (16, 8, LANES))
    out_ref[...] = jnp.concatenate(
        [features[:, 0], packed, features[:, 1], packed], axis=1
    ).astype(jnp.bfloat16)


def attend(query, key_cache, value_cache, lengths):
    width = key_cache.shape[1] * key_cache.shape[2]
    keys = key_cache.reshape(SEQS, width, LANES)
    values = value_cache.reshape(SEQS, width, LANES)
    vmem = pl.BlockSpec(memory_space=pltpu.VMEM)
    hbm = pl.BlockSpec(memory_space=pltpu.HBM)
    return pl.pallas_call(
        attend_kernel,
        out_shape=jax.ShapeDtypeStruct((16, 48, LANES), jnp.bfloat16),
        in_specs=[hbm] * 4,
        out_specs=vmem,
        scratch_shapes=[
            pltpu.SMEM((SEQS,), jnp.int32),
            pltpu.VMEM((SEQS, HEADS, LANES), jnp.bfloat16),
            pltpu.VMEM((SEQS, width, LANES), jnp.bfloat16),
            pltpu.VMEM((SEQS, width, LANES), jnp.bfloat16),
            pltpu.VMEM((512, LANES), jnp.float32),
            pltpu.VMEM((512, LANES), jnp.float32),
            pltpu.SemaphoreType.DMA((2,)),
            pltpu.SemaphoreType.DMA((SEQS,)),
            pltpu.SemaphoreType.DMA((SEQS,)),
        ],
        compiler_params=pltpu.CompilerParams(vmem_limit_bytes=60 * 1024 * 1024),
        cost_estimate=pl.CostEstimate(
            flops=270_000_000, bytes_accessed=8_800_000, transcendentals=540_000
        ),
    )(lengths, query, keys, values)


def split_kernel(own_ref, other_ref, out_ref):
    core = lax.axis_index("core")
    for t in range(own_ref.shape[2] // 512):
        start = pl.multiple_of(t * 512 + core * 256, 256)
        for which, ref in ((core, own_ref), (1 - core, other_ref)):
            rows = pl.ds(pl.multiple_of(which * 64, 64), 64)
            piece = ref[:, :, pl.ds(start, 256)]
            out_ref[rows, t * 256 : (t + 1) * 256] = piece.reshape(64, 256)


def split_weight(own, other):
    vmem = pl.BlockSpec(memory_space=pltpu.VMEM)
    return pl.pallas_call(
        split_kernel,
        out_shape=jax.ShapeDtypeStruct((LANES, HALF), jnp.bfloat16),
        in_specs=[vmem, vmem],
        out_specs=vmem,
        compiler_params=pltpu.CompilerParams(vmem_limit_bytes=16 * 1024 * 1024),
        cost_estimate=pl.CostEstimate(flops=0, bytes_accessed=4_194_304, transcendentals=0),
    )(own, other)


def local(query, key_cache, value_cache, lengths, out_weight):
    packed = attend(query, key_cache, value_cache, lengths)
    packed, out_weight = lax.optimization_barrier((packed, out_weight))
    got = lax.all_to_all(
        packed.reshape(32, 24, LANES), "chip", split_axis=0, concat_axis=0, tiled=True
    )
    other = lax.ppermute(out_weight, "core", [(0, 1), (1, 0)])
    weight = split_weight(out_weight, other)

    part = merge(got.reshape(16, 48, LANES))
    other_part = lax.ppermute(part, "core", [(0, 1), (1, 0)])
    terms = project(part, other_part, weight)
    terms = lax.all_to_all(
        terms.reshape(128, 8, LANES), ("chip", "tp"), split_axis=0, concat_axis=0, tiled=True
    )
    return final_sum(terms.reshape(64, 16, LANES))


def solution(mesh):
    parts = Mesh(mesh.devices.reshape(32, 2, 4), ("chip", "core", "tp"))
    placed = (
        P(None, "tp", None),
        P(None, ("chip", "core"), "tp", None),
        P(None, ("chip", "core"), "tp", None),
        P(),
        P("tp", ("chip", "core"), None),
    )
    return jax.shard_map(
        local,
        mesh=parts,
        in_specs=placed,
        out_specs=P(None, ("chip", "core", "tp")),
        check_vma=False,
    )
```

```python
import functools

import jax
import jax.numpy as jnp
import numpy as np
from jax import lax
from jax.experimental import pallas as pl
from jax.experimental.pallas import tpu as pltpu
from jax.sharding import Mesh
from jax.sharding import PartitionSpec as P

SEQS = 16
HEADS = 32
LANES = 128
CHIP_FEATURES = 4
HALF = 8192
CUTS = (0, 4, 9, 13, 16)
AHEAD = 4


def spread_table():
    table = np.zeros((CHIP_FEATURES, 4, HEADS, LANES), np.float32)
    for i in range(CHIP_FEATURES):
        for h in range(HEADS):
            table[i, :, h, (i // 2) * 64 + h * 2 + i % 2] = 1.0
    return table.reshape(4 * LANES, LANES)


def repeat_table():
    table = np.zeros((4, 4, 4, 16), np.float32)
    for i in range(4):
        for k in range(4):
            table[i, k, :, i * 4 + k] = 1.0
    return table.reshape(64, 16)


def merge_kernel(got_ref, out_ref):
    got = got_ref[...].astype(jnp.float32).reshape(32, 24, LANES)
    stats = got[:, 16:24]
    swapped = pltpu.roll(stats, 4, 1)
    upper = lax.broadcasted_iota(jnp.int32, stats.shape, 1) < 4
    coarse = jnp.where(upper, stats, swapped)
    fine = jnp.where(upper, swapped, stats)
    highest = jnp.max(coarse, axis=0)
    scale = jnp.exp(coarse - highest[None])
    out_ref[0:8] = jnp.sum(scale * got[:, 0:8], axis=0)
    out_ref[8:16] = jnp.sum(scale * got[:, 8:16], axis=0)
    out_ref[16:24] = highest
    out_ref[24:32] = jnp.sum(scale * fine, axis=0)


def merge(got):
    vmem = pl.BlockSpec(memory_space=pltpu.VMEM)
    return pl.pallas_call(
        merge_kernel,
        out_shape=jax.ShapeDtypeStruct((32, LANES), jnp.float32),
        in_specs=[vmem],
        out_specs=vmem,
        compiler_params=pltpu.CompilerParams(vmem_limit_bytes=16 * 1024 * 1024),
        cost_estimate=pl.CostEstimate(flops=400_000, bytes_accessed=212_992, transcendentals=32768),
    )(got)


def project_kernel(own_ref, other_ref, weight_ref, spread_ref, repeat_ref, out_ref):
    highest = jnp.maximum(own_ref[16:24], other_ref[16:24])
    own_scale = jnp.exp(own_ref[16:24] - highest)
    other_scale = jnp.exp(other_ref[16:24] - highest)
    total = own_scale * own_ref[24:32] + other_scale * other_ref[24:32]
    first = (own_scale * own_ref[0:8] + other_scale * other_ref[0:8]) / total
    second = (own_scale * own_ref[8:16] + other_scale * other_ref[8:16]) / total
    merged = jnp.concatenate([first, second], axis=0).astype(jnp.bfloat16)
    rows = jnp.dot(repeat_ref[...], merged, preferred_element_type=jnp.float32)
    lane_group = lax.broadcasted_iota(jnp.int32, rows.shape, 1) // 32
    row_group = lax.broadcasted_iota(jnp.int32, rows.shape, 0) % 4
    rows = jnp.where(lane_group == row_group, rows, 0.0).astype(jnp.bfloat16)
    wide = jnp.concatenate([rows[16 * i : 16 * i + 16] for i in range(4)], axis=1)
    left = jnp.dot(wide, spread_ref[...], preferred_element_type=jnp.float32).astype(jnp.bfloat16)
    low = lax.broadcasted_iota(jnp.int32, (8, LANES), 1) < 64
    step = 1024
    for start in range(0, HALF, step):
        part = jnp.dot(
            left, weight_ref[:, start : start + step], preferred_element_type=jnp.float32
        )
        for tile in range(step // LANES):
            piece = part[:, tile * LANES : (tile + 1) * LANES]
            top, bottom = piece[0:8], piece[8:16]
            even = jnp.where(low, top, pltpu.roll(bottom, 64, 1))
            odd = jnp.where(low, pltpu.roll(top, 64, 1), bottom)
            out_ref[start // LANES + tile] = jnp.concatenate([even, odd], axis=0).astype(
                jnp.bfloat16
            )


def project(own, other, weight):
    vmem = pl.BlockSpec(memory_space=pltpu.VMEM)
    return pl.pallas_call(
        project_kernel,
        out_shape=jax.ShapeDtypeStruct((HALF // LANES, 16, LANES), jnp.bfloat16),
        in_specs=[vmem] * 5,
        out_specs=vmem,
        compiler_params=pltpu.CompilerParams(vmem_limit_bytes=24 * 1024 * 1024),
        cost_estimate=pl.CostEstimate(flops=34_000_000, bytes_accessed=3_000_000, transcendentals=65536),
    )(
        own,
        other,
        weight,
        jnp.asarray(spread_table(), jnp.bfloat16),
        jnp.asarray(repeat_table(), jnp.bfloat16),
    )


def final_sum_kernel(got_ref, out_ref):
    total = jnp.sum(got_ref[...].astype(jnp.float32), axis=0)
    total = total[0:8] + total[8:16]
    out_ref[...] = jnp.concatenate([total[:, 0:64], total[:, 64:128]], axis=0).astype(jnp.bfloat16)


def final_sum(got):
    vmem = pl.BlockSpec(memory_space=pltpu.VMEM)
    return pl.pallas_call(
        final_sum_kernel,
        out_shape=jax.ShapeDtypeStruct((SEQS, 64), jnp.bfloat16),
        in_specs=[vmem],
        out_specs=vmem,
        compiler_params=pltpu.CompilerParams(vmem_limit_bytes=16 * 1024 * 1024),
        cost_estimate=pl.CostEstimate(flops=131072, bytes_accessed=264192, transcendentals=0),
    )(got)


def attend_kernel(
    lengths_hbm,
    query_hbm,
    key_hbm,
    value_hbm,
    out_ref,
    lengths_ref,
    query_ref,
    keys,
    values,
    outs,
    turned,
    small_sem,
    key_sem,
    value_sem,
):
    width = key_hbm.shape[1]
    block_index = lax.axis_index("chip") * 2 + lax.axis_index("core")
    base = block_index * (width // 2)
    query_copy = pltpu.make_async_copy(query_hbm, query_ref, small_sem.at[0])
    lengths_copy = pltpu.make_async_copy(lengths_hbm, lengths_ref, small_sem.at[1])
    groups = [range(a, b) for a, b in zip(CUTS[:-1], CUTS[1:])]
    key_copies = []
    value_copies = []
    for t, group in enumerate(groups):
        rows = pl.ds(group.start, len(group))
        key_copies.append(pltpu.make_async_copy(key_hbm.at[rows], keys.at[rows], key_sem.at[t]))
        value_copies.append(
            pltpu.make_async_copy(value_hbm.at[rows], values.at[rows], value_sem.at[t])
        )
    query_copy.start()
    lengths_copy.start()
    loads = []
    for t in range(len(groups) + 1):
        if t < len(groups):
            loads.append(key_copies[t])
        if t > 0:
            loads.append(value_copies[t - 1])
    for copy in loads[:AHEAD]:
        copy.start()
    begun, used = AHEAD, 0

    column = lax.broadcasted_iota(jnp.int32, (HEADS, width), 1)
    row = lax.broadcasted_iota(jnp.int32, (HEADS, width), 0)
    position = jnp.where((column % 2) == (row // 16), column // 2, jnp.int32(1 << 30))
    lane = lax.broadcasted_iota(jnp.int32, (HEADS, LANES), 1)
    factor = jnp.float32(LANES**-0.5)
    query_copy.wait()
    lengths_copy.wait()
    scores, weights, ratios, stats = {}, {}, {}, [0.0] * 4
    for t in range(len(groups) + 2):
        first = groups[t] if t < len(groups) else ()
        second = groups[t - 1] if 1 <= t <= len(groups) else ()
        third = groups[t - 2] if t >= 2 else ()
        if first:
            key_copies[t].wait()
        if third:
            value_copies[t - 2].wait()
        used += (len(first) > 0) + (len(third) > 0)
        for copy in loads[begun : used + AHEAD]:
            copy.start()
        begun = max(begun, used + AHEAD)
        for b in first:
            raw = lax.dot_general(
                query_ref[b],
                keys[b],
                (((1,), (1,)), ((), ())),
                preferred_element_type=jnp.float32,
            )
            scores[b] = jnp.where(position < lengths_ref[b] - base, raw, jnp.float32(-1e30))
        for b in third:
            summed = jnp.dot(weights[b], values[b], preferred_element_type=jnp.float32)
            outs[b * HEADS : b * HEADS + HEADS] = summed * ratios[b]
            k = b // 4
            if b % 4 == 3:
                turned[pl.ds(k, LANES, stride=4), :] = outs[k * LANES : k * LANES + LANES].T
        for b in second:
            top = jnp.max(scores[b], axis=1, keepdims=True)
            weight = jnp.exp2((scores[b] - top) * (factor * jnp.float32(1.4426950408889634)))
            total = jnp.sum(weight, axis=1, keepdims=True)
            weights[b] = weight.astype(jnp.bfloat16)
            top = top * factor
            coarse = (top + jnp.log(total)).astype(jnp.bfloat16).astype(jnp.float32)
            fine = total * jnp.exp(top - coarse)
            fine = fine.astype(jnp.bfloat16).astype(jnp.float32)
            fine = jnp.where(lengths_ref[b] > base, fine, 0.0)
            ratios[b] = fine / total
            k = b // 4
            stats[b % 4] = jnp.where(
                lane == k, coarse, jnp.where(lane == k + 4, fine, stats[b % 4])
            )
        if t == len(groups):
            packed = jnp.concatenate(stats, axis=0).T[0:8]
    features = turned[...].reshape(16, 2, 16, LANES)
    packed = jnp.broadcast_to(packed[None], (16, 8, LANES))
    out_ref[...] = jnp.concatenate(
        [features[:, 0], packed, features[:, 1], packed], axis=1
    ).astype(jnp.bfloat16)


def attend(query, key_cache, value_cache, lengths):
    width = key_cache.shape[1] * key_cache.shape[2]
    keys = key_cache.reshape(SEQS, width, LANES)
    values = value_cache.reshape(SEQS, width, LANES)
    vmem = pl.BlockSpec(memory_space=pltpu.VMEM)
    hbm = pl.BlockSpec(memory_space=pltpu.HBM)
    return pl.pallas_call(
        attend_kernel,
        out_shape=jax.ShapeDtypeStruct((16, 48, LANES), jnp.bfloat16),
        in_specs=[hbm] * 4,
        out_specs=vmem,
        scratch_shapes=[
            pltpu.SMEM((SEQS,), jnp.int32),
            pltpu.VMEM((SEQS, HEADS, LANES), jnp.bfloat16),
            pltpu.VMEM((SEQS, width, LANES), jnp.bfloat16),
            pltpu.VMEM((SEQS, width, LANES), jnp.bfloat16),
            pltpu.VMEM((512, LANES), jnp.float32),
            pltpu.VMEM((512, LANES), jnp.float32),
            pltpu.SemaphoreType.DMA((2,)),
            pltpu.SemaphoreType.DMA((SEQS,)),
            pltpu.SemaphoreType.DMA((SEQS,)),
        ],
        compiler_params=pltpu.CompilerParams(vmem_limit_bytes=60 * 1024 * 1024),
        cost_estimate=pl.CostEstimate(
            flops=270_000_000, bytes_accessed=8_800_000, transcendentals=540_000
        ),
    )(lengths, query, keys, values)


def split_kernel(own_ref, other_ref, out_ref):
    core = lax.axis_index("core")
    for t in range(own_ref.shape[2] // 512):
        start = pl.multiple_of(t * 512 + core * 256, 256)
        for which, ref in ((core, own_ref), (1 - core, other_ref)):
            rows = pl.ds(pl.multiple_of(which * 64, 64), 64)
            piece = ref[:, :, pl.ds(start, 256)]
            out_ref[rows, t * 256 : (t + 1) * 256] = piece.reshape(64, 256)


def split_weight(own, other):
    vmem = pl.BlockSpec(memory_space=pltpu.VMEM)
    return pl.pallas_call(
        split_kernel,
        out_shape=jax.ShapeDtypeStruct((LANES, HALF), jnp.bfloat16),
        in_specs=[vmem, vmem],
        out_specs=vmem,
        compiler_params=pltpu.CompilerParams(vmem_limit_bytes=16 * 1024 * 1024),
        cost_estimate=pl.CostEstimate(flops=0, bytes_accessed=4_194_304, transcendentals=0),
    )(own, other)


def local(query, key_cache, value_cache, lengths, out_weight):
    packed = attend(query, key_cache, value_cache, lengths)
    packed, out_weight = lax.optimization_barrier((packed, out_weight))
    got = lax.all_to_all(
        packed.reshape(32, 24, LANES), "chip", split_axis=0, concat_axis=0, tiled=True
    )
    other = lax.ppermute(out_weight, "core", [(0, 1), (1, 0)])
    weight = split_weight(out_weight, other)

    part = merge(got.reshape(16, 48, LANES))
    other_part = lax.ppermute(part, "core", [(0, 1), (1, 0)])
    terms = project(part, other_part, weight)
    terms = lax.all_to_all(
        terms.reshape(128, 8, LANES), ("chip", "tp"), split_axis=0, concat_axis=0, tiled=True
    )
    return final_sum(terms.reshape(64, 16, LANES))


def solution(mesh):
    parts = Mesh(mesh.devices.reshape(32, 2, 4), ("chip", "core", "tp"))
    placed = (
        P(None, "tp", None),
        P(None, ("chip", "core"), "tp", None),
        P(None, ("chip", "core"), "tp", None),
        P(),
        P("tp", ("chip", "core"), None),
    )
    return jax.shard_map(
        local,
        mesh=parts,
        in_specs=placed,
        out_specs=P(None, ("chip", "core", "tp")),
        check_vma=False,
    )
```

```python
import functools

import jax
import jax.numpy as jnp
import numpy as np
from jax import lax
from jax.experimental import pallas as pl
from jax.experimental.pallas import tpu as pltpu
from jax.sharding import Mesh
from jax.sharding import PartitionSpec as P

SEQS = 16
HEADS = 32
LANES = 128
CHIP_FEATURES = 4
HALF = 8192
CUTS = (0, 4, 9, 13, 16)
AHEAD = 4


def spread_table():
    table = np.zeros((CHIP_FEATURES, 4, HEADS, LANES), np.float32)
    for i in range(CHIP_FEATURES):
        for h in range(HEADS):
            table[i, :, h, (i // 2) * 64 + h * 2 + i % 2] = 1.0
    return table.reshape(4 * LANES, LANES)


def repeat_table():
    table = np.zeros((4, 4, 4, 16), np.float32)
    for i in range(4):
        for k in range(4):
            table[i, k, :, i * 4 + k] = 1.0
    return table.reshape(64, 16)


def merge_kernel(got_ref, out_ref):
    got = got_ref[...].astype(jnp.float32).reshape(32, 24, LANES)
    stats = got[:, 16:24]
    swapped = pltpu.roll(stats, 4, 1)
    upper = lax.broadcasted_iota(jnp.int32, stats.shape, 1) < 4
    coarse = jnp.where(upper, stats, swapped)
    fine = jnp.where(upper, swapped, stats)
    highest = jnp.max(coarse, axis=0)
    scale = jnp.exp(coarse - highest[None])
    out_ref[0:8] = jnp.sum(scale * got[:, 0:8], axis=0)
    out_ref[8:16] = jnp.sum(scale * got[:, 8:16], axis=0)
    out_ref[16:24] = highest
    out_ref[24:32] = jnp.sum(scale * fine, axis=0)


def merge(got):
    vmem = pl.BlockSpec(memory_space=pltpu.VMEM)
    return pl.pallas_call(
        merge_kernel,
        out_shape=jax.ShapeDtypeStruct((32, LANES), jnp.float32),
        in_specs=[vmem],
        out_specs=vmem,
        compiler_params=pltpu.CompilerParams(vmem_limit_bytes=16 * 1024 * 1024),
        cost_estimate=pl.CostEstimate(flops=400_000, bytes_accessed=212_992, transcendentals=32768),
    )(got)


def project_kernel(own_ref, other_ref, weight_ref, spread_ref, repeat_ref, out_ref):
    highest = jnp.maximum(own_ref[16:24], other_ref[16:24])
    own_scale = jnp.exp(own_ref[16:24] - highest)
    other_scale = jnp.exp(other_ref[16:24] - highest)
    total = own_scale * own_ref[24:32] + other_scale * other_ref[24:32]
    first = (own_scale * own_ref[0:8] + other_scale * other_ref[0:8]) / total
    second = (own_scale * own_ref[8:16] + other_scale * other_ref[8:16]) / total
    merged = jnp.concatenate([first, second], axis=0).astype(jnp.bfloat16)
    rows = jnp.dot(repeat_ref[...], merged, preferred_element_type=jnp.float32)
    lane_group = lax.broadcasted_iota(jnp.int32, rows.shape, 1) // 32
    row_group = lax.broadcasted_iota(jnp.int32, rows.shape, 0) % 4
    rows = jnp.where(lane_group == row_group, rows, 0.0).astype(jnp.bfloat16)
    wide = jnp.concatenate([rows[16 * i : 16 * i + 16] for i in range(4)], axis=1)
    left = jnp.dot(wide, spread_ref[...], preferred_element_type=jnp.float32).astype(jnp.bfloat16)
    low = lax.broadcasted_iota(jnp.int32, (8, LANES), 1) < 64
    step = 2048
    for start in range(0, HALF, step):
        part = jnp.dot(
            left, weight_ref[:, start : start + step], preferred_element_type=jnp.float32
        )
        for tile in range(step // LANES):
            piece = part[:, tile * LANES : (tile + 1) * LANES]
            top, bottom = piece[0:8], piece[8:16]
            even = jnp.where(low, top, pltpu.roll(bottom, 64, 1))
            odd = jnp.where(low, pltpu.roll(top, 64, 1), bottom)
            out_ref[start // LANES + tile] = jnp.concatenate([even, odd], axis=0).astype(
                jnp.bfloat16
            )


def project(own, other, weight):
    vmem = pl.BlockSpec(memory_space=pltpu.VMEM)
    return pl.pallas_call(
        project_kernel,
        out_shape=jax.ShapeDtypeStruct((HALF // LANES, 16, LANES), jnp.bfloat16),
        in_specs=[vmem] * 5,
        out_specs=vmem,
        compiler_params=pltpu.CompilerParams(vmem_limit_bytes=24 * 1024 * 1024),
        cost_estimate=pl.CostEstimate(flops=34_000_000, bytes_accessed=3_000_000, transcendentals=65536),
    )(
        own,
        other,
        weight,
        jnp.asarray(spread_table(), jnp.bfloat16),
        jnp.asarray(repeat_table(), jnp.bfloat16),
    )


def final_sum_kernel(got_ref, out_ref):
    total = jnp.sum(got_ref[...].astype(jnp.float32), axis=0)
    total = total[0:8] + total[8:16]
    out_ref[...] = jnp.concatenate([total[:, 0:64], total[:, 64:128]], axis=0).astype(jnp.bfloat16)


def final_sum(got):
    vmem = pl.BlockSpec(memory_space=pltpu.VMEM)
    return pl.pallas_call(
        final_sum_kernel,
        out_shape=jax.ShapeDtypeStruct((SEQS, 64), jnp.bfloat16),
        in_specs=[vmem],
        out_specs=vmem,
        compiler_params=pltpu.CompilerParams(vmem_limit_bytes=16 * 1024 * 1024),
        cost_estimate=pl.CostEstimate(flops=131072, bytes_accessed=264192, transcendentals=0),
    )(got)


def attend_kernel(
    lengths_hbm,
    query_hbm,
    key_hbm,
    value_hbm,
    out_ref,
    lengths_ref,
    query_ref,
    keys,
    values,
    outs,
    turned,
    small_sem,
    key_sem,
    value_sem,
):
    width = key_hbm.shape[1]
    block_index = lax.axis_index("chip") * 2 + lax.axis_index("core")
    base = block_index * (width // 2)
    query_copy = pltpu.make_async_copy(query_hbm, query_ref, small_sem.at[0])
    lengths_copy = pltpu.make_async_copy(lengths_hbm, lengths_ref, small_sem.at[1])
    groups = [range(a, b) for a, b in zip(CUTS[:-1], CUTS[1:])]
    key_copies = []
    value_copies = []
    for t, group in enumerate(groups):
        rows = pl.ds(group.start, len(group))
        key_copies.append(pltpu.make_async_copy(key_hbm.at[rows], keys.at[rows], key_sem.at[t]))
        value_copies.append(
            pltpu.make_async_copy(value_hbm.at[rows], values.at[rows], value_sem.at[t])
        )
    query_copy.start()
    lengths_copy.start()
    loads = []
    for t in range(len(groups) + 1):
        if t < len(groups):
            loads.append(key_copies[t])
        if t > 0:
            loads.append(value_copies[t - 1])
    for copy in loads[:AHEAD]:
        copy.start()
    begun, used = AHEAD, 0

    column = lax.broadcasted_iota(jnp.int32, (HEADS, width), 1)
    row = lax.broadcasted_iota(jnp.int32, (HEADS, width), 0)
    position = jnp.where((column % 2) == (row // 16), column // 2, jnp.int32(1 << 30))
    lane = lax.broadcasted_iota(jnp.int32, (HEADS, LANES), 1)
    factor = jnp.float32(LANES**-0.5)
    query_copy.wait()
    lengths_copy.wait()
    scores, weights, ratios, stats = {}, {}, {}, [0.0] * 4
    for t in range(len(groups) + 2):
        first = groups[t] if t < len(groups) else ()
        second = groups[t - 1] if 1 <= t <= len(groups) else ()
        third = groups[t - 2] if t >= 2 else ()
        if first:
            key_copies[t].wait()
        if third:
            value_copies[t - 2].wait()
        used += (len(first) > 0) + (len(third) > 0)
        for copy in loads[begun : used + AHEAD]:
            copy.start()
        begun = max(begun, used + AHEAD)
        for b in first:
            raw = lax.dot_general(
                query_ref[b],
                keys[b],
                (((1,), (1,)), ((), ())),
                preferred_element_type=jnp.float32,
            )
            scores[b] = jnp.where(position < lengths_ref[b] - base, raw, jnp.float32(-1e30))
        for b in third:
            summed = jnp.dot(weights[b], values[b], preferred_element_type=jnp.float32)
            outs[b * HEADS : b * HEADS + HEADS] = summed * ratios[b]
            k = b // 4
            if b % 4 == 3:
                turned[pl.ds(k, LANES, stride=4), :] = outs[k * LANES : k * LANES + LANES].T
        for b in second:
            top = jnp.max(scores[b], axis=1, keepdims=True)
            weight = jnp.exp2((scores[b] - top) * (factor * jnp.float32(1.4426950408889634)))
            total = jnp.sum(weight, axis=1, keepdims=True)
            weights[b] = weight.astype(jnp.bfloat16)
            top = top * factor
            coarse = (top + jnp.log(total)).astype(jnp.bfloat16).astype(jnp.float32)
            fine = total * jnp.exp(top - coarse)
            fine = fine.astype(jnp.bfloat16).astype(jnp.float32)
            fine = jnp.where(lengths_ref[b] > base, fine, 0.0)
            ratios[b] = fine / total
            k = b // 4
            stats[b % 4] = jnp.where(
                lane == k, coarse, jnp.where(lane == k + 4, fine, stats[b % 4])
            )
        if t == len(groups):
            packed = jnp.concatenate(stats, axis=0).T[0:8]
    features = turned[...].reshape(16, 2, 16, LANES)
    packed = jnp.broadcast_to(packed[None], (16, 8, LANES))
    out_ref[...] = jnp.concatenate(
        [features[:, 0], packed, features[:, 1], packed], axis=1
    ).astype(jnp.bfloat16)


def attend(query, key_cache, value_cache, lengths):
    width = key_cache.shape[1] * key_cache.shape[2]
    keys = key_cache.reshape(SEQS, width, LANES)
    values = value_cache.reshape(SEQS, width, LANES)
    vmem = pl.BlockSpec(memory_space=pltpu.VMEM)
    hbm = pl.BlockSpec(memory_space=pltpu.HBM)
    return pl.pallas_call(
        attend_kernel,
        out_shape=jax.ShapeDtypeStruct((16, 48, LANES), jnp.bfloat16),
        in_specs=[hbm] * 4,
        out_specs=vmem,
        scratch_shapes=[
            pltpu.SMEM((SEQS,), jnp.int32),
            pltpu.VMEM((SEQS, HEADS, LANES), jnp.bfloat16),
            pltpu.VMEM((SEQS, width, LANES), jnp.bfloat16),
            pltpu.VMEM((SEQS, width, LANES), jnp.bfloat16),
            pltpu.VMEM((512, LANES), jnp.float32),
            pltpu.VMEM((512, LANES), jnp.float32),
            pltpu.SemaphoreType.DMA((2,)),
            pltpu.SemaphoreType.DMA((SEQS,)),
            pltpu.SemaphoreType.DMA((SEQS,)),
        ],
        compiler_params=pltpu.CompilerParams(vmem_limit_bytes=60 * 1024 * 1024),
        cost_estimate=pl.CostEstimate(
            flops=270_000_000, bytes_accessed=8_800_000, transcendentals=540_000
        ),
    )(lengths, query, keys, values)


def split_kernel(own_ref, other_ref, out_ref):
    core = lax.axis_index("core")
    for t in range(own_ref.shape[2] // 512):
        start = pl.multiple_of(t * 512 + core * 256, 256)
        for which, ref in ((core, own_ref), (1 - core, other_ref)):
            rows = pl.ds(pl.multiple_of(which * 64, 64), 64)
            piece = ref[:, :, pl.ds(start, 256)]
            out_ref[rows, t * 256 : (t + 1) * 256] = piece.reshape(64, 256)


def split_weight(own, other):
    vmem = pl.BlockSpec(memory_space=pltpu.VMEM)
    return pl.pallas_call(
        split_kernel,
        out_shape=jax.ShapeDtypeStruct((LANES, HALF), jnp.bfloat16),
        in_specs=[vmem, vmem],
        out_specs=vmem,
        compiler_params=pltpu.CompilerParams(vmem_limit_bytes=16 * 1024 * 1024),
        cost_estimate=pl.CostEstimate(flops=0, bytes_accessed=4_194_304, transcendentals=0),
    )(own, other)


def local(query, key_cache, value_cache, lengths, out_weight):
    packed = attend(query, key_cache, value_cache, lengths)
    packed, out_weight = lax.optimization_barrier((packed, out_weight))
    got = lax.all_to_all(
        packed.reshape(32, 24, LANES), "chip", split_axis=0, concat_axis=0, tiled=True
    )
    other = lax.ppermute(out_weight, "core", [(0, 1), (1, 0)])
    weight = split_weight(out_weight, other)

    part = merge(got.reshape(16, 48, LANES))
    other_part = lax.ppermute(part, "core", [(0, 1), (1, 0)])
    terms = project(part, other_part, weight)
    terms = lax.all_to_all(
        terms.reshape(128, 8, LANES), ("chip", "tp"), split_axis=0, concat_axis=0, tiled=True
    )
    return final_sum(terms.reshape(64, 16, LANES))


def solution(mesh):
    parts = Mesh(mesh.devices.reshape(32, 2, 4), ("chip", "core", "tp"))
    placed = (
        P(None, "tp", None),
        P(None, ("chip", "core"), "tp", None),
        P(None, ("chip", "core"), "tp", None),
        P(),
        P("tp", ("chip", "core"), None),
    )
    return jax.shard_map(
        local,
        mesh=parts,
        in_specs=placed,
        out_specs=P(None, ("chip", "core", "tp")),
        check_vma=False,
    )
```
